32 devices in a mesh: groups: 2 (over y), scan: 4 (over z), stripe: 2 (over x), sub: 2 (over core).
Axes of the slice: x: 2, y: 2, z: 4, core: 2. Of those that a mesh axis runs over, the one named last changes fastest.
Arguments:
- object_field: float32 [2, 2048, 1024], P(None, ('groups', 'stripe', 'sub'), 'scan'), parts along dimension 1, may hold values from -6 to 6
- probe_field: float32 [2, 256, 128], P(None, 'groups'), parts along dimension 1, may hold values from -6 to 6
- intensity: float32 [512, 128, 128], P(('groups', 'scan', 'stripe', 'sub')), parts along dimension 0, may hold values from 0 to 2
- positions: int32 [512, 2], P(('groups', 'scan', 'stripe', 'sub')), parts along dimension 0, may hold values from 0 to 128
- owner_tile: int32 [512, 1], P(('groups', 'scan', 'stripe', 'sub')), parts along dimension 0, may hold values from 0 to 3; in each aligned block of 16 rows (0 to 15, 16 to 31, ...) at most 8 rows name the same one
Outputs:
- object_grad: float32 [2, 2048, 1024], P(None, ('groups', 'stripe', 'sub'), 'scan'), parts along dimension 1
- probe_grad: float32 [2, 256, 128], P(None, 'groups'), parts along dimension 1
The draws below stay inside these ranges and needn't reach their ends.
There are 2 independent parts, one for each index of `groups`. The reference program is written for one: setup_inputs(seed, part) draws one part's arguments, and reference() takes and returns one part's arrays. A program takes and returns all parts, laid end to end along the dimension named above; each array names one. Nothing has to cross between parts.
Inputs may be any that keep to these rules, and one draw needn't show every extreme that they name: `owner_tile`: among the 16 patterns of one device no tile column is named more than 8 times, and on some device one column is named exactly 8 times. `positions`: every window lies wholly inside its owning tile.
All inputs are finite; a program needn't handle non-finite values.
Results may differ from the reference program's by a relative error of at most 0.0001.
Values sent between devices are 32-bit elements; how exact they have to be, the bound alone decides.
A program may use at most 64 MiB of HBM per device.

```python
import math
import jax
import jax.numpy as jnp
import numpy as np
from jax import lax

W = 128
TILE = 256
PAT_DEV = 16
CAP = 8
NR = 1024
NC = 1024
PATTERNS = 256
N_SCAN = 4
N_STRIPE = 2
N_SUB = 2


def touch_ends(entries, key, low, high):
    index_at = [jax.random.randint(jax.random.fold_in(key, axis), (), 0, length) for axis, length in enumerate(entries.shape)]
    longest = entries.shape.index(max(entries.shape))
    next_to = index_at[:longest] + [(index_at[longest] + 1) % entries.shape[longest]] + index_at[longest + 1:]
    return entries.at[tuple(index_at)].set(low).at[tuple(next_to)].set(high)


def levels(own_key, dims, shards, least, high):
    gain, own = 1.0, jax.random.fold_in(own_key, 6)
    for position, shards_of in shards:
        heights = jnp.exp(jax.random.uniform(jax.random.fold_in(own, position), (shards_of,), jnp.float32, least / len(shards), high / len(shards)))
        gain = gain * jnp.repeat(heights, dims[position] // shards_of).reshape([-1 if axis == position else 1 for axis in range(len(dims))])
    return gain


def shared_out(own_key, own, number, rows, count, top, most, slope):
    order = jax.random.permutation(own_key, count)
    packed, usual = portions_of(count, rows * top, most, slope, True), portions_of(count, rows * top, most, slope, False)
    places = jnp.arange(count)

    def named(tallies, offset_by):
        used = int((tallies > 0).sum())
        fixed = max(1, used // 4)
        moved = fixed + (places - fixed + offset_by * (used - fixed)) % max(1, count - fixed)
        return jnp.zeros((count,), jnp.int32).at[order[jnp.where(places < fixed, places, moved)]].set(jnp.asarray(tallies, jnp.int32))

    tallies = jnp.where(number % 4 == 0, named(packed, number // 4), named(usual, number - number // 4 - 1))
    mixed = jax.random.permutation(jax.random.fold_in(own, 3), count)
    source_of, sink = mixed[0:count // 2 * 2:2], mixed[1:count // 2 * 2:2]
    margin = jnp.minimum(tallies[source_of] - 1, most - tallies[sink]) // 2
    margin = jnp.where((source_of == order[0]) | (sink == order[0]) | (tallies[sink] == 0), 0, jnp.maximum(margin, 0))
    moved = jax.random.randint(jax.random.fold_in(own, 4), (count // 2,), 0, 1 << 20) % (margin + 1)
    tallies = tallies.at[source_of].add(-moved).at[sink].add(moved)
    items = jnp.searchsorted(jnp.cumsum(tallies), jnp.arange(rows * top), side="right").astype(jnp.int32)
    listing = items.reshape(top, rows).T
    listing = listing[jax.random.permutation(jax.random.fold_in(own, 1), rows)]
    offset_by = jax.random.randint(jax.random.fold_in(own, 2), (rows, 1), 0, top)
    return jnp.take_along_axis(listing, (jnp.arange(top)[None, :] + offset_by) % top, axis=1)


def portions_of(number_of, total, reach, skew, full):
    portions = [(1 << 20) // math.isqrt(rank ** skew) + 1 for rank in range(1, number_of + 1)]
    largest = reach if full else min(reach, max(-(-total // number_of), total * portions[0] // sum(portions)))
    least = 1 if total - largest >= number_of - 1 else 0
    holding, surplus = [largest] + [least] * (number_of - 1), total - largest - least * (number_of - 1)
    while surplus > 0:
        candidates = [i for i in range(1, number_of) if holding[i] < largest] or [i for i in range(1, number_of) if holding[i] < reach]
        pool, budget = sum([portions[i] for i in candidates]), surplus
        for i in candidates:
            more = min(reach - holding[i], max(1, budget * portions[i] // pool), surplus)
            holding[i] = holding[i] + more
            surplus = surplus - more
    return np.array(holding)


def normal_values(rng, extent, scale, bound, cuts=(), held_as=jnp.bfloat16):
    entries = scale * jax.random.normal(rng, extent, jnp.float32)
    if cuts:
        entries = entries * levels(rng, extent, cuts, -0.22, 0.18)
    return jnp.clip(entries, -bound, bound).astype(held_as)


def setup_inputs(seed: int = 0, part: int = 0) -> dict:
    streams_of = jax.random.split(jax.random.key(seed), 6)
    own_keys = jax.random.split(jax.random.fold_in(streams_of[5], part), 6)
    object_field = normal_values(own_keys[0], (2, NR, NC), 0.7, 6.0, ((1, 4), (2, 4)), jnp.float32)
    probe_field = normal_values(own_keys[1], (2, W, W), 0.7, 6.0, (), jnp.float32)
    intensity = jnp.clip(2.0 * jax.random.uniform(own_keys[2], (PATTERNS, W, W), jnp.float32) ** levels(own_keys[2], (PATTERNS, W, W), ((0, 16),), -0.2, 0.2), 0.0, 2.0)
    positions = touch_ends(jax.random.randint(own_keys[3], (PATTERNS, 2), 0, TILE - W + 1), jax.random.fold_in(own_keys[3], 1), 0, TILE - W).astype(jnp.int32)
    owner_tile_keys = jax.random.split(jax.random.fold_in(own_keys[4], 1), PATTERNS // PAT_DEV)
    owner_tile_turns = jax.random.permutation(jax.random.fold_in(own_keys[4], 3), PATTERNS // PAT_DEV)
    owner_tile = jax.vmap(lambda own, number: shared_out(jax.random.fold_in(own_keys[4], 2), own, number, PAT_DEV, N_SCAN, 1, CAP, 2))(owner_tile_keys, owner_tile_turns).reshape((PATTERNS, 1))
    return dict(object_field=object_field, probe_field=probe_field, intensity=intensity, positions=positions, owner_tile=owner_tile)


def cut_windows(source, rows_at, cols_at):
    def single(row_one, col_one):
        return lax.dynamic_slice(source, (jnp.zeros((), jnp.int32), row_one, col_one), (2, W, W))
    return jax.vmap(single)(rows_at, cols_at)


def gradients(windows, probe_field, measured):
    crop_re, crop_im = windows[:, 0], windows[:, 1]
    probe_re, probe_im = probe_field[0], probe_field[1]
    exit_re = probe_re * crop_re - probe_im * crop_im
    exit_im = probe_re * crop_im + probe_im * crop_re
    far_field = jnp.fft.fft2(exit_re + 1j * exit_im, norm="ortho")
    far_re = jnp.real(far_field)
    far_im = jnp.imag(far_field)
    misfit = far_re ** 2 + far_im ** 2 - measured
    back_wave = jnp.fft.ifft2(misfit * far_re + 1j * (misfit * far_im), norm="ortho")
    back_re = jnp.real(back_wave)
    back_im = jnp.imag(back_wave)
    object_term = jnp.stack([probe_re * back_re + probe_im * back_im, probe_re * back_im - probe_im * back_re], axis=1)
    probe_term = jnp.stack([crop_re * back_re + crop_im * back_im, crop_re * back_im - crop_im * back_re], axis=1)
    return object_term, probe_term


def reference(object_field, probe_field, intensity, positions, owner_tile):
    band_count = N_STRIPE * N_SUB
    block_count = PATTERNS // PAT_DEV
    pattern_ids = jnp.arange(PATTERNS, dtype=jnp.int32)
    band_of = (pattern_ids // PAT_DEV) % band_count
    rows_at = (band_of * TILE + positions[:, 0]).astype(jnp.int32)
    cols_at = (owner_tile[:, 0] * TILE + positions[:, 1]).astype(jnp.int32)

    def block_step(carried, pieces):
        grad_field, probe_total = carried
        rows_blk, cols_blk, measured = pieces
        windows = cut_windows(object_field, rows_blk, cols_blk)
        object_term, probe_term = gradients(windows, probe_field, measured)

        def paste_one(index, target):
            corner = (jnp.zeros((), jnp.int32), rows_blk[index], cols_blk[index])
            current = lax.dynamic_slice(target, corner, (2, W, W))
            return lax.dynamic_update_slice(target, current + object_term[index], corner)

        grad_field = lax.fori_loop(0, PAT_DEV, paste_one, grad_field)
        return (grad_field, probe_total + jnp.sum(probe_term, axis=0)), None

    initial = (jnp.zeros_like(object_field), jnp.zeros((2, W, W), jnp.float32))
    (grad_field, probe_total), unused = lax.scan(block_step, initial, (rows_at.reshape(block_count, PAT_DEV), cols_at.reshape(block_count, PAT_DEV), intensity.reshape(block_count, PAT_DEV, W, W)))
    return grad_field, probe_total / PAT_DEV
```

```python
import functools
import math

import jax
import jax.numpy as jnp
import ml_dtypes
import numpy as np
from jax import lax
from jax.experimental import pallas as pl
from jax.experimental.pallas import tpu as pltpu
from jax.sharding import PartitionSpec as P

MESH = pl.DeviceIdType.MESH


def tables(extent):
    counter = np.arange(extent)
    angles = (counter[:, None] * counter[None, :] % extent) * (2.0 * math.pi / extent)
    c, s = np.cos(angles) / math.sqrt(extent), -np.sin(angles) / math.sqrt(extent)
    parts = []
    for whole in (np.block([[c, s], [-s, c]]), np.block([[c, -s], [s, c]])):
        high = whole.astype(np.float32).astype(ml_dtypes.bfloat16)
        low = (whole - high.astype(np.float64)).astype(np.float32).astype(ml_dtypes.bfloat16)
        parts += [high, low]
    return np.stack(parts)


def split(x):
    high = x.astype(jnp.bfloat16)
    return high, (x - high.astype(jnp.float32)).astype(jnp.bfloat16)


def dot(a, b):
    return jnp.dot(a, b, preferred_element_type=jnp.float32)


def dot_right(x, high, low):
    x_high, x_low = split(x)
    return dot(x_high, high) + dot(x_low, high) + dot(x_high, low)


def dot_left(high, low, x):
    x_high, x_low = split(x)
    return dot(high, x_high) + dot(high, x_low) + dot(low, x_high)


def kernel(
    sizes, table_sm, table_vm, inten, obj, probe, dft, grad, probe_out,
    send, recv, meta_in, meta, field, pad, total, reduced, gathered, arrived,
    send_sem, recv_sem, meta_send_sem, meta_recv_sem, local_sem,
    rs_send, rs_recv, ag_send, ag_recv,
):
    n, stripes, subs, cap, batch, offsets = sizes
    groups = cap // batch
    extent = inten.shape[1]
    tile = obj.shape[1]
    halves = tile // extent
    members = n * stripes * subs
    rows = arrived.shape[1]
    owners = 2 * extent // rows
    my_group, me = lax.axis_index("groups"), lax.axis_index("scan")
    my_stripe, my_sub = lax.axis_index("stripe"), lax.axis_index("sub")
    mine = (me * stripes + my_stripe) * subs + my_sub

    def member(place):
        return (my_group, place // (stripes * subs), place // subs % stripes, place % subs)

    def other(step):
        return lax.rem(mine + step, members)

    barrier = pltpu.get_barrier_semaphore()

    def greet(step, carry):
        pl.semaphore_signal(barrier, inc=1, device_id=member(other(step)), device_id_type=MESH)
        return carry

    lax.fori_loop(1, members, greet, 0)

    def pack(o, target, into):
        def one(slot, carry):
            into[o, slot] = inten[table_sm[target, 0, slot]]
            return carry

        lax.fori_loop(0, cap, one, 0)

    def data_copy(o, g, target):
        part = pl.ds(g * batch, batch)
        return pltpu.make_async_remote_copy(
            src_ref=send.at[o, part], dst_ref=recv.at[o, part],
            send_sem=send_sem, recv_sem=recv_sem.at[o, g],
            device_id=(my_group, target, my_stripe, my_sub), device_id_type=MESH,
        )

    def meta_copy(o, target):
        return pltpu.make_async_remote_copy(
            src_ref=table_vm.at[target], dst_ref=meta_in.at[o],
            send_sem=meta_send_sem, recv_sem=meta_recv_sem.at[o],
            device_id=(my_group, target, my_stripe, my_sub), device_id_type=MESH,
        )

    targets = [lax.rem(me + offset, n) for offset in offsets]
    for o in range(1, n):
        pack(o, targets[o], send)
    pl.semaphore_wait(barrier, members - 1)
    for o in range(1, n):
        meta_copy(o, targets[o]).start()
    for o in range(1, n):
        for g in range(groups):
            data_copy(o, g, targets[o]).start()
    own = pltpu.make_async_copy(table_vm.at[me], meta.at[0], local_sem)
    own.start()
    pack(0, me, recv)
    own.wait()

    for h in range(halves):
        field[:, h] = obj[:, :, h * extent:(h + 1) * extent]
    grad[...] = jnp.zeros_like(grad)
    total[...] = jnp.zeros_like(total)
    pad[...] = jnp.zeros_like(pad)

    def step_of(i, carry):
        o, g = i // groups, i % groups

        @pl.when((o > 0) & (g == 0))
        def _():
            meta_copy(o, me).wait_recv()
            down = pltpu.make_async_copy(meta_in.at[o], meta.at[o], local_sem)
            down.start()
            down.wait()

        @pl.when(o > 0)
        def _():
            data_copy(o, g, me).wait_recv()

        corners, crops, exits = [], [], []
        pr, pi = probe[0], probe[1]
        for b in range(batch):
            slot = g * batch + b
            row, col = meta[o, 0, cap + slot], meta[o, 0, 2 * cap + slot]
            weight = jnp.where(meta[o, 0, 3 * cap + slot] > 0, 1.0, 0.0).astype(jnp.float32)
            corners.append((row, col, weight))
            back_by = lax.rem(tile - col, tile)
            cr, ci = [
                pltpu.roll(
                    jnp.concatenate([field[c, h, pl.ds(row, extent), :] for h in range(halves)], axis=1), back_by, 1
                )[:, :extent]
                for c in range(2)
            ]
            crops.append((cr, ci))
            exits.append(jnp.concatenate([pr * cr - pi * ci, pr * ci + pi * cr], axis=1))
        y = dot_right(jnp.concatenate(exits, axis=0), dft[0], dft[1])

        def turn(x):
            return jnp.concatenate(
                [
                    jnp.concatenate(
                        [x[b * extent:(b + 1) * extent, c * extent:(c + 1) * extent] for b in range(batch)], axis=1
                    )
                    for c in range(2)
                ],
                axis=0,
            )

        z = dot_left(dft[2], dft[3], turn(y))
        re, im = z[:extent], z[extent:]
        measured = jnp.concatenate([recv[o, g * batch + b] for b in range(batch)], axis=1)
        misfit = re * re + im * im - measured
        v = dot_left(dft[0], dft[1], jnp.concatenate([misfit * re, misfit * im], axis=0))
        turned = jnp.concatenate(
            [
                jnp.concatenate(
                    [v[c * extent:(c + 1) * extent, b * extent:(b + 1) * extent] for c in range(2)], axis=1
                )
                for b in range(batch)
            ],
            axis=0,
        )
        back = dot_right(turned, dft[2], dft[3])
        sum_re, sum_im = total[:extent], total[extent:]
        nothing = jnp.zeros((extent, tile - extent), jnp.float32)
        for b in range(batch):
            row, col, weight = corners[b]
            cr, ci = crops[b]
            br = back[b * extent:(b + 1) * extent, :extent] * weight
            bi = back[b * extent:(b + 1) * extent, extent:] * weight
            sum_re += cr * br + ci * bi
            sum_im += cr * bi - ci * br
            for c, term in enumerate((pr * br + pi * bi, pr * bi - pi * br)):
                wide = pltpu.roll(jnp.concatenate([term, nothing], axis=1), col, 1)
                for h in range(halves):
                    pad[b, c, h, tile - extent:tile, :] = wide[:, h * extent:(h + 1) * extent]
        total[:extent] = sum_re
        total[extent:] = sum_im
        for c in range(2):
            for start in range(0, tile, 64):
                for h in range(halves):
                    held = grad[c, start:start + 64, h * extent:(h + 1) * extent]
                    for b in range(batch):
                        held += pad[b, c, h, pl.ds(tile - extent - corners[b][0] + start, 64), :]
                    grad[c, start:start + 64, h * extent:(h + 1) * extent] = held
        return carry

    lax.fori_loop(0, n * groups, step_of, 0)

    def when(condition, body):
        if owners == members:
            body()
        else:
            pl.when(condition)(body)

    def part_of(place):
        return pl.ds(pl.multiple_of(place * rows, rows), rows)

    def scatter(step, carry):
        to = other(step)

        def go():
            pltpu.make_async_remote_copy(
                src_ref=total.at[part_of(to)], dst_ref=arrived.at[step - 1], send_sem=rs_send, recv_sem=rs_recv,
                device_id=member(to), device_id_type=MESH,
            ).start()

        when(to < owners, go)
        return carry

    def wait_for(sem, count):
        whole = arrived.at[pl.ds(0, count)]
        pltpu.make_async_copy(whole, whole, sem).wait()

    lax.fori_loop(1, members, scatter, 0)

    def gather():
        wait_for(rs_recv, members - 1)
        held = total[part_of(mine), :]
        held = held + jnp.sum(arrived[...], axis=0)
        reduced[...] = held * (1.0 / inten.shape[0])
        gathered[mine] = reduced[...]

        def tell(step, carry):
            pltpu.make_async_remote_copy(
                src_ref=reduced, dst_ref=gathered.at[mine], send_sem=ag_send, recv_sem=ag_recv,
                device_id=member(other(step)), device_id_type=MESH,
            ).start()
            return carry

        lax.fori_loop(1, members, tell, 0)

    when(mine < owners, gather)
    if owners == members:
        wait_for(ag_recv, members - 1)
        wait_for(rs_send, members - 1)
        wait_for(ag_send, members - 1)
    else:

        @pl.when(mine < owners)
        def _():
            wait_for(ag_recv, owners - 1)
            wait_for(rs_send, owners - 1)
            wait_for(ag_send, members - 1)

        @pl.when(mine >= owners)
        def _():
            wait_for(ag_recv, owners)
            wait_for(rs_send, owners)

    for place in range(owners):
        probe_out[place * rows:(place + 1) * rows] = gathered[place]
    sent = send.at[pl.ds(1, n - 1)]
    pltpu.make_async_copy(sent, sent, send_sem).wait()
    told = meta_in.at[pl.ds(1, n - 1)]
    pltpu.make_async_copy(told, told, meta_send_sem).wait()


def shards(object_field, probe_field, intensity, positions, owner_tile):
    n, stripes, subs = lax.axis_size("scan"), lax.axis_size("stripe"), lax.axis_size("sub")
    count, extent = intensity.shape[0], probe_field.shape[1]
    tile = object_field.shape[1]
    cap = min(count, 2 * count // n)
    batch = min(cap, 4)
    members = n * stripes * subs
    rows = max(8, 2 * extent // members)
    owners = 2 * extent // rows

    owner = owner_tile[:, 0]
    places = jnp.arange(count, dtype=jnp.int32)
    rank = jnp.sum((owner[:, None] == owner[None, :]) & (places[None, :] < places[:, None]), axis=1, dtype=jnp.int32)
    named = jnp.arange(n, dtype=jnp.int32)[:, None, None, None] == owner
    ranked = jnp.arange(cap, dtype=jnp.int32)[:, None] == rank
    facts = jnp.stack([places, positions[:, 0], positions[:, 1], jnp.ones_like(places)])[:, None, :]
    table = jnp.sum(jnp.where(named & ranked, facts, 0), axis=3, dtype=jnp.int32).reshape(n, 1, 4 * cap)
    table = jnp.pad(table, ((0, 0), (0, 0), (0, 128 - 4 * cap)))

    offsets = sorted(range(n), key=lambda o: (o != 0, o))
    vmem = pl.BlockSpec(memory_space=pltpu.VMEM)
    dma = pltpu.SemaphoreType.DMA
    f32 = jnp.float32
    grad, probe_grad = pl.pallas_call(
        functools.partial(kernel, (n, stripes, subs, cap, batch, tuple(offsets))),
        out_shape=(
            jax.ShapeDtypeStruct((2, tile, tile), f32),
            jax.ShapeDtypeStruct((2 * extent, extent), f32),
        ),
        in_specs=[pl.BlockSpec(memory_space=pltpu.SMEM)] + [vmem] * 5,
        out_specs=(vmem, vmem),
        scratch_shapes=[
            pltpu.VMEM((n, cap, extent, extent), f32),
            pltpu.VMEM((n, cap, extent, extent), f32),
            pltpu.VMEM((n, 1, 128), jnp.int32),
            pltpu.SMEM((n, 1, 128), jnp.int32),
            pltpu.VMEM((2, tile // extent, tile, extent), f32),
            pltpu.VMEM((batch, 2, tile // extent, 2 * tile - extent, extent), f32),
            pltpu.VMEM((2 * extent, extent), f32),
            pltpu.VMEM((rows, extent), f32),
            pltpu.VMEM((owners, rows, extent), f32),
            pltpu.VMEM((members - 1, rows, extent), f32),
            dma, dma((n, cap // batch)), dma, dma((n,)), dma, dma, dma, dma, dma,
        ],
        compiler_params=pltpu.CompilerParams(
            collective_id=0, has_side_effects=True, vmem_limit_bytes=40 * 1024 * 1024
        ),
        cost_estimate=pl.CostEstimate(
            flops=3 * 4 * 2 * 256 * 256 * 128 * n * cap, bytes_accessed=8 * 1024 * 1024, transcendentals=0
        ),
    )(table, table, intensity, object_field, probe_field, jnp.asarray(tables(extent)))
    return grad, probe_grad.reshape(2, extent, extent)


def solution(mesh):
    in_specs = (
        P(None, ("groups", "stripe", "sub"), "scan"),
        P(None, "groups", None),
        P(("groups", "scan", "stripe", "sub"), None, None),
        P(("groups", "scan", "stripe", "sub"), None),
        P(("groups", "scan", "stripe", "sub"), None),
    )
    out_specs = (P(None, ("groups", "stripe", "sub"), "scan"), P(None, "groups", None))
    return jax.shard_map(shards, mesh=mesh, in_specs=in_specs, out_specs=out_specs, check_vma=False)
```

```python
import functools
import math

import jax
import jax.numpy as jnp
import numpy as np
from jax import lax
from jax.experimental import pallas as pl
from jax.experimental.pallas import tpu as pltpu
from jax.sharding import PartitionSpec as P

MESH = pl.DeviceIdType.MESH
AHEAD = 4


def tables(extent):
    counter = np.arange(extent)
    angles = (counter[:, None] * counter[None, :] % extent) * (2.0 * math.pi / extent)
    return (np.stack([np.cos(angles), -np.sin(angles)]) / math.sqrt(extent)).astype(np.float32)


def other_place(me, mask, n):
    if n & (n - 1):
        return lax.rem(me + mask, n)
    place, bit = 0, 1
    while bit < n:
        place = place + bit * ((me // bit + mask // bit) % 2)
        bit *= 2
    return place


def split(x):
    high = x.astype(jnp.bfloat16)
    return high, (x - high.astype(jnp.float32)).astype(jnp.bfloat16)


def dot(a, b):
    return jnp.dot(a, b, preferred_element_type=jnp.float32)


def dot_right(x, high, low):
    x_high, x_low = split(x)
    return dot(x_high, high) + dot(x_low, high) + dot(x_high, low)


def dot_left(high, low, x):
    x_high, x_low = split(x)
    return dot(high, x_high) + dot(high, x_low) + dot(low, x_high)


def kernel(
    sizes, places_hbm, owner_hbm, inten_hbm, obj, probe_hbm, waves_hbm, grad, probe_out,
    inten, probe, waves, dft, send, recv, places_in, owner_in, places, owner, field, pad, total, reduced, gathered, arrived,
    in_sem, send_sem, recv_sem, meta_send_sem, meta_recv_sem, local_sem,
    rs_send, rs_recv, ag_send, ag_recv,
):
    n, stripes, subs, cap, batch = sizes
    groups = cap // batch
    extent = inten.shape[1]
    tile = obj.shape[1]
    halves = tile // extent
    members = n * stripes * subs
    rows = arrived.shape[1]
    owners = 2 * extent // rows
    my_group, me = lax.axis_index("groups"), lax.axis_index("scan")
    my_stripe, my_sub = lax.axis_index("stripe"), lax.axis_index("sub")
    mine = (me * stripes + my_stripe) * subs + my_sub

    def member(place):
        return (my_group, place // (stripes * subs), place // subs % stripes, place % subs)

    def other(step):
        return lax.rem(mine + step, members)

    def each_member(body):
        lax.fori_loop(1, members, body, 0, unroll=members <= 16)

    barrier = pltpu.get_barrier_semaphore()

    def greet(step, carry):
        pl.semaphore_signal(barrier, inc=1, device_id=member(other(step)), device_id_type=MESH)
        return carry

    own = [
        pltpu.make_async_copy(places_hbm, places.at[0], local_sem.at[0]),
        pltpu.make_async_copy(owner_hbm, owner.at[0], local_sem.at[1]),
    ]
    for copy in own:
        copy.start()
    fetch = pltpu.make_async_copy(inten_hbm, inten, in_sem.at[0])
    fetch.start()
    later = [
        pltpu.make_async_copy(obj.at[:, :, pl.ds(h * extent, extent)], field.at[:, h], in_sem.at[3 + h])
        for h in range(halves)
    ]
    later += [
        pltpu.make_async_copy(probe_hbm, probe, in_sem.at[1]),
        pltpu.make_async_copy(waves_hbm, waves, in_sem.at[2]),
    ]
    for copy in later:
        copy.start()
    each_member(greet)

    def find(o, target, slot):
        index, seen = jnp.int32(0), jnp.int32(0)
        for j in range(inten.shape[0]):
            hit = owner[o, 0, j] == target
            index = jnp.where(hit & (seen == slot), j, index)
            seen = seen + jnp.where(hit, 1, 0)
        return index, seen > slot

    def pack(o, g, target, into):
        for b in range(batch):
            slot = g * batch + b
            into[o, slot] = inten[find(0, target, slot)[0]]

    def data_copy(o, g, target):
        part = pl.ds(g * batch, batch)
        return pltpu.make_async_remote_copy(
            src_ref=send.at[o, part], dst_ref=recv.at[o, part],
            send_sem=send_sem.at[o, g], recv_sem=recv_sem.at[o, g],
            device_id=(my_group, target, my_stripe, my_sub), device_id_type=MESH,
        )

    def meta_copies(o, target):
        return [
            pltpu.make_async_remote_copy(
                src_ref=src, dst_ref=dst.at[o],
                send_sem=meta_send_sem.at[k, o], recv_sem=meta_recv_sem.at[k, o],
                device_id=(my_group, target, my_stripe, my_sub), device_id_type=MESH,
            )
            for k, (src, dst) in enumerate(((places_hbm, places_in), (owner_hbm, owner_in)))
        ]

    targets = [other_place(me, o, n) for o in range(n)]
    ahead = min(AHEAD, (n - 1) * groups)

    def turn_of(i):
        return 1 + (i + 1) % (n - 1), i // (n - 1)

    for copy in own:
        copy.wait()
    fetch.wait()
    pack(*turn_of(0), targets[turn_of(0)[0]], send)
    pl.semaphore_wait(barrier, members - 1)
    for o in range(1, n):
        for copy in meta_copies(o, targets[o]):
            copy.start()
    for i in range((n - 1) * groups):
        o, g = turn_of(i)
        if i:
            pack(o, g, targets[o], send)
        if i < ahead:
            data_copy(o, g, targets[o]).start()
    for g in range(groups):
        pack(0, g, me, recv)
    for copy in later:
        copy.wait()
    for k, sign in enumerate((1.0, -1.0)):
        c, s = waves[0], waves[1] * sign
        high, low = split(jnp.concatenate([jnp.concatenate([c, s], 1), jnp.concatenate([-s, c], 1)], 0))
        dft[2 * k] = high
        dft[2 * k + 1] = low

    grad[...] = jnp.zeros_like(grad)
    total[...] = jnp.zeros_like(total)
    pad[...] = jnp.zeros_like(pad)

    def step_of(j, carry):
        i = j - groups
        o = jnp.where(i < 0, 0, 1 + (i + 1) % (n - 1))
        g = jnp.where(i < 0, j, i // (n - 1))

        @pl.when((i >= 0) & (i + ahead < (n - 1) * groups))
        def _():
            data_copy(o, g, me).wait_send()
            next_o, next_g = turn_of(i + ahead)
            to = other_place(me, next_o, n)
            data_copy(next_o, next_g, to).start()

        @pl.when((o > 0) & (g == 0))
        def _():
            for copy in meta_copies(o, me):
                copy.wait_recv()
            down = [
                pltpu.make_async_copy(places_in.at[o], places.at[o], local_sem.at[0]),
                pltpu.make_async_copy(owner_in.at[o], owner.at[o], local_sem.at[1]),
            ]
            for copy in down:
                copy.start()
            for copy in down:
                copy.wait()

        @pl.when(o > 0)
        def _():
            data_copy(o, g, me).wait_recv()

        corners, crops, exits = [], [], []
        pr, pi = probe[0], probe[1]
        for b in range(batch):
            slot = g * batch + b
            index, is_there = find(o, me, slot)
            row, col = places[o, 0, index], places[o, 1, index]
            weight = jnp.where(is_there, 1.0, 0.0).astype(jnp.float32)
            corners.append((row, col, weight))
            back_by = lax.rem(tile - col, tile)
            cr, ci = [
                pltpu.roll(
                    jnp.concatenate([field[c, h, pl.ds(row, extent), :] for h in range(halves)], axis=1), back_by, 1
                )[:, :extent]
                for c in range(2)
            ]
            crops.append((cr, ci))
            exits.append(jnp.concatenate([pr * cr - pi * ci, pr * ci + pi * cr], axis=1))
        y = dot_right(jnp.concatenate(exits, axis=0), dft[0], dft[1])

        def turn(x):
            return jnp.concatenate(
                [
                    jnp.concatenate(
                        [x[b * extent:(b + 1) * extent, c * extent:(c + 1) * extent] for b in range(batch)], axis=1
                    )
                    for c in range(2)
                ],
                axis=0,
            )

        z = dot_left(dft[2], dft[3], turn(y))
        re, im = z[:extent], z[extent:]
        measured = jnp.concatenate([recv[o, g * batch + b] for b in range(batch)], axis=1)
        misfit = re * re + im * im - measured
        v = dot_left(dft[0], dft[1], jnp.concatenate([misfit * re, misfit * im], axis=0))
        turned = jnp.concatenate(
            [
                jnp.concatenate(
                    [v[c * extent:(c + 1) * extent, b * extent:(b + 1) * extent] for c in range(2)], axis=1
                )
                for b in range(batch)
            ],
            axis=0,
        )
        back = dot_right(turned, dft[2], dft[3])
        sum_re, sum_im = total[:extent], total[extent:]
        nothing = jnp.zeros((extent, tile - extent), jnp.float32)
        for b in range(batch):
            row, col, weight = corners[b]
            cr, ci = crops[b]
            br = back[b * extent:(b + 1) * extent, :extent] * weight
            bi = back[b * extent:(b + 1) * extent, extent:] * weight
            sum_re += cr * br + ci * bi
            sum_im += cr * bi - ci * br
            for c, term in enumerate((pr * br + pi * bi, pr * bi - pi * br)):
                wide = pltpu.roll(jnp.concatenate([term, nothing], axis=1), col, 1)
                for h in range(halves):
                    pad[b, c, h, tile - extent:tile, :] = wide[:, h * extent:(h + 1) * extent]
        total[:extent] = sum_re
        total[extent:] = sum_im
        for c in range(2):
            for start in range(0, tile, 64):
                for h in range(halves):
                    held = grad[c, start:start + 64, h * extent:(h + 1) * extent]
                    for b in range(batch):
                        held += pad[b, c, h, pl.ds(tile - extent - corners[b][0] + start, 64), :]
                    grad[c, start:start + 64, h * extent:(h + 1) * extent] = held
        return carry

    lax.fori_loop(0, n * groups, step_of, 0)

    def when(condition, body):
        if owners == members:
            body()
        else:
            pl.when(condition)(body)

    def part_of(place):
        return pl.ds(pl.multiple_of(place * rows, rows), rows)

    def scatter(step, carry):
        to = other(step)

        def go():
            pltpu.make_async_remote_copy(
                src_ref=total.at[part_of(to)], dst_ref=arrived.at[step - 1], send_sem=rs_send, recv_sem=rs_recv,
                device_id=member(to), device_id_type=MESH,
            ).start()

        when(to < owners, go)
        return carry

    def wait_for(sem, count):
        whole = arrived.at[pl.ds(0, count)]
        pltpu.make_async_copy(whole, whole, sem).wait()

    each_member(scatter)

    def gather():
        wait_for(rs_recv, members - 1)
        held = total[part_of(mine), :]
        held = held + jnp.sum(arrived[...], axis=0)
        reduced[...] = held * (1.0 / inten.shape[0])
        gathered[mine] = reduced[...]

        def tell(step, carry):
            pltpu.make_async_remote_copy(
                src_ref=reduced, dst_ref=gathered.at[mine], send_sem=ag_send, recv_sem=ag_recv,
                device_id=member(other(step)), device_id_type=MESH,
            ).start()
            return carry

        each_member(tell)

    when(mine < owners, gather)
    if owners == members:
        wait_for(ag_recv, members - 1)
        wait_for(rs_send, members - 1)
        wait_for(ag_send, members - 1)
    else:

        @pl.when(mine < owners)
        def _():
            wait_for(ag_recv, owners - 1)
            wait_for(rs_send, owners - 1)
            wait_for(ag_send, members - 1)

        @pl.when(mine >= owners)
        def _():
            wait_for(ag_recv, owners)
            wait_for(rs_send, owners)

    for place in range(owners):
        probe_out[place * rows:(place + 1) * rows] = gathered[place]
    for i in range((n - 1) * groups - ahead, (n - 1) * groups):
        data_copy(*turn_of(i), me).wait_send()
    for o in range(1, n):
        for copy in meta_copies(o, me):
            copy.wait_send()


def shards(object_field, probe_field, intensity, positions, owner_tile):
    n, stripes, subs = lax.axis_size("scan"), lax.axis_size("stripe"), lax.axis_size("sub")
    count, extent = intensity.shape[0], probe_field.shape[1]
    tile = object_field.shape[1]
    cap = min(count, 2 * count // n)
    batch = min(cap, 2)
    members = n * stripes * subs
    rows = max(8, 2 * extent // members)
    owners = 2 * extent // rows

    hbm = pl.BlockSpec(memory_space=pltpu.HBM)
    vmem = pl.BlockSpec(memory_space=pltpu.VMEM)
    dma = pltpu.SemaphoreType.DMA
    f32 = jnp.float32
    grad, probe_grad = pl.pallas_call(
        functools.partial(kernel, (n, stripes, subs, cap, batch)),
        out_shape=(
            jax.ShapeDtypeStruct((2, tile, tile), f32),
            jax.ShapeDtypeStruct((2 * extent, extent), f32),
        ),
        in_specs=[hbm] * 6,
        out_specs=(vmem, vmem),
        scratch_shapes=[
            pltpu.VMEM(intensity.shape, f32),
            pltpu.VMEM(probe_field.shape, f32),
            pltpu.VMEM((2, extent, extent), f32),
            pltpu.VMEM((4, 2 * extent, 2 * extent), jnp.bfloat16),
            pltpu.VMEM((n, cap, extent, extent), f32),
            pltpu.VMEM((n, cap, extent, extent), f32),
            pltpu.VMEM((n, 2, count), jnp.int32),
            pltpu.VMEM((n, 1, count), jnp.int32),
            pltpu.SMEM((n, 2, count), jnp.int32),
            pltpu.SMEM((n, 1, count), jnp.int32),
            pltpu.VMEM((2, tile // extent, tile, extent), f32),
            pltpu.VMEM((batch, 2, tile // extent, 2 * tile - extent, extent), f32),
            pltpu.VMEM((2 * extent, extent), f32),
            pltpu.VMEM((rows, extent), f32),
            pltpu.VMEM((owners, rows, extent), f32),
            pltpu.VMEM((members - 1, rows, extent), f32),
            dma((3 + tile // extent,)), dma((n, cap // batch)), dma((n, cap // batch)), dma((2, n)), dma((2, n)), dma((2,)), dma, dma, dma, dma,
        ],
        compiler_params=pltpu.CompilerParams(
            collective_id=0, has_side_effects=True, vmem_limit_bytes=64 * 1024 * 1024
        ),
        cost_estimate=pl.CostEstimate(
            flops=3 * 4 * 2 * 256 * 256 * 128 * n * cap, bytes_accessed=8 * 1024 * 1024, transcendentals=0
        ),
    )(positions.T, owner_tile.T, intensity, object_field, probe_field, jnp.asarray(tables(extent)))
    return grad, probe_grad.reshape(2, extent, extent)


def solution(mesh):
    in_specs = (
        P(None, ("groups", "stripe", "sub"), "scan"),
        P(None, "groups", None),
        P(("groups", "scan", "stripe", "sub"), None, None),
        P(("groups", "scan", "stripe", "sub"), None),
        P(("groups", "scan", "stripe", "sub"), None),
    )
    out_specs = (P(None, ("groups", "stripe", "sub"), "scan"), P(None, "groups", None))
    return jax.shard_map(shards, mesh=mesh, in_specs=in_specs, out_specs=out_specs, check_vma=False)
```

```python
import functools
import math

import jax
import jax.numpy as jnp
import numpy as np
from jax import lax
from jax.experimental import pallas as pl
from jax.experimental.pallas import tpu as pltpu
from jax.sharding import PartitionSpec as P

MESH = pl.DeviceIdType.MESH
AHEAD = 3


def tables(extent):
    counter = np.arange(extent)
    angles = (counter[:, None] * counter[None, :] % extent) * (2.0 * math.pi / extent)
    return (np.stack([np.cos(angles), -np.sin(angles)]) / math.sqrt(extent)).astype(np.float32)


def other_place(me, mask, n):
    if n & (n - 1):
        return lax.rem(me + mask, n)
    place, bit = 0, 1
    while bit < n:
        place = place + bit * ((me // bit + mask // bit) % 2)
        bit *= 2
    return place


def split(x):
    high = x.astype(jnp.bfloat16)
    return high, (x - high.astype(jnp.float32)).astype(jnp.bfloat16)


def dot(a, b):
    return jnp.dot(a, b, preferred_element_type=jnp.float32)


def dot_right(x, high, low):
    x_high, x_low = split(x)
    return dot(x_high, high) + dot(x_low, high) + dot(x_high, low)


def dot_left(high, low, x):
    x_high, x_low = split(x)
    return dot(high, x_high) + dot(high, x_low) + dot(low, x_high)


def kernel(
    sizes, places_hbm, owner_hbm, inten_hbm, obj, probe_hbm, waves_hbm, grad_hbm, probe_out,
    grad, inten, probe, waves, dft, send, recv, places_in, owner_in, places, owner, field, pad, total, reduced, gathered, arrived,
    in_sem, send_sem, recv_sem, meta_send_sem, meta_recv_sem, local_sem,
    rs_send, rs_recv, ag_send, ag_recv,
):
    n, stripes, subs, cap, batch = sizes
    groups = cap // batch
    extent = inten.shape[1]
    tile = obj.shape[1]
    halves = tile // extent
    members = n * stripes * subs
    rows = arrived.shape[1]
    owners = 2 * extent // rows
    my_group, me = lax.axis_index("groups"), lax.axis_index("scan")
    my_stripe, my_sub = lax.axis_index("stripe"), lax.axis_index("sub")
    mine = (me * stripes + my_stripe) * subs + my_sub

    def member(place):
        return (my_group, place // (stripes * subs), place // subs % stripes, place % subs)

    def other(step):
        return lax.rem(mine + step, members)

    def each_member(body):
        lax.fori_loop(1, members, body, 0, unroll=members <= 16)

    barrier = pltpu.get_barrier_semaphore()

    def greet(step, carry):
        pl.semaphore_signal(barrier, inc=1, device_id=member(other(step)), device_id_type=MESH)
        return carry

    own = [
        pltpu.make_async_copy(places_hbm, places.at[0], local_sem.at[0]),
        pltpu.make_async_copy(owner_hbm, owner.at[0], local_sem.at[1]),
    ]
    for copy in own:
        copy.start()
    fetch = pltpu.make_async_copy(inten_hbm, inten, in_sem.at[0])
    fetch.start()
    later = [
        pltpu.make_async_copy(obj.at[:, :, pl.ds(h * extent, extent)], field.at[:, h], in_sem.at[3 + h])
        for h in range(halves)
    ]
    later += [
        pltpu.make_async_copy(probe_hbm, probe, in_sem.at[1]),
        pltpu.make_async_copy(waves_hbm, waves, in_sem.at[2]),
    ]
    for copy in later:
        copy.start()
    each_member(greet)

    def find(o, target, slot):
        index, seen = jnp.int32(0), jnp.int32(0)
        for j in range(inten.shape[0]):
            hit = owner[o, 0, j] == target
            index = jnp.where(hit & (seen == slot), j, index)
            seen = seen + jnp.where(hit, 1, 0)
        return index, seen > slot

    def pack(o, g, target, into):
        for b in range(batch):
            slot = g * batch + b
            into[o, slot] = inten[find(0, target, slot)[0]]

    def data_copy(o, g, target):
        part = pl.ds(g * batch, batch)
        return pltpu.make_async_remote_copy(
            src_ref=send.at[o, part], dst_ref=recv.at[o, part],
            send_sem=send_sem.at[o, g], recv_sem=recv_sem.at[o, g],
            device_id=(my_group, target, my_stripe, my_sub), device_id_type=MESH,
        )

    def meta_copies(o, target):
        return [
            pltpu.make_async_remote_copy(
                src_ref=src, dst_ref=dst.at[o],
                send_sem=meta_send_sem.at[k, o], recv_sem=meta_recv_sem.at[k, o],
                device_id=(my_group, target, my_stripe, my_sub), device_id_type=MESH,
            )
            for k, (src, dst) in enumerate(((places_hbm, places_in), (owner_hbm, owner_in)))
        ]

    targets = [other_place(me, o, n) for o in range(n)]
    total_steps = n // 2 * groups

    def pair_of(i):
        return [(i // groups * 2 + side, i % groups) for side in range(2)]

    for copy in own:
        copy.wait()
    fetch.wait()
    early = [(1, g) for g in range(groups)]
    queue = [turn for i in range(groups, total_steps) for turn in pair_of(i)]
    early = [turn for turns in zip(queue, early) for turn in turns]
    first = early + [turn for turn in queue[:2 * AHEAD] if turn not in early]
    late = [turn for turn in queue if turn not in first]
    pack(*first[0][:2], targets[first[0][0]], send)
    pl.semaphore_wait(barrier, members - 1)
    for o in range(1, n):
        for copy in meta_copies(o, targets[o]):
            copy.start()
    for o, g in first:
        if (o, g) != first[0]:
            pack(o, g, targets[o], send)
        data_copy(o, g, targets[o]).start()
    for o, g in late:
        pack(o, g, targets[o], send)
    for g in range(groups):
        pack(0, g, me, recv)
    for copy in later:
        copy.wait()
    for k, sign in enumerate((1.0, -1.0)):
        c, s = waves[0], waves[1] * sign
        high, low = split(jnp.concatenate([jnp.concatenate([c, s], 1), jnp.concatenate([-s, c], 1)], 0))
        dft[2 * k] = high
        dft[2 * k + 1] = low

    grad[...] = jnp.zeros_like(grad)
    total[...] = jnp.zeros_like(total)
    pad[...] = jnp.zeros_like(pad)

    def step_of(j, carry):
        pair = j // groups
        g = j % groups

        @pl.when((j >= groups) & (j + AHEAD < total_steps))
        def _():
            for turn in pair_of(j):
                data_copy(*turn, me).wait_send()
            for o, later_g in pair_of(j + AHEAD):
                data_copy(o, later_g, other_place(me, o, n)).start()

        def settle(o):
            @pl.when(g == 0)
            def _():
                for copy in meta_copies(o, me):
                    copy.wait_recv()
                down = [
                    pltpu.make_async_copy(places_in.at[o], places.at[o], local_sem.at[0]),
                    pltpu.make_async_copy(owner_in.at[o], owner.at[o], local_sem.at[1]),
                ]
                for copy in down:
                    copy.start()
                for copy in down:
                    copy.wait()

            data_copy(o, g, me).wait_recv()

        pl.when(pair > 0)(lambda: settle(pair * 2))
        settle(pair * 2 + 1)

        corners, crops, exits = [], [], []
        pr, pi = probe[0], probe[1]
        turns = [(pair * 2 + b % 2, g * batch + b // 2) for b in range(2 * batch)]
        for o, slot in turns:
            index, is_there = find(o, me, slot)
            row, col = places[o, 0, index], places[o, 1, index]
            weight = jnp.where(is_there, 1.0, 0.0).astype(jnp.float32)
            corners.append((row, col, weight))
            back_by = lax.rem(tile - col, tile)
            cr, ci = [
                pltpu.roll(
                    jnp.concatenate([field[c, h, pl.ds(row, extent), :] for h in range(halves)], axis=1), back_by, 1
                )[:, :extent]
                for c in range(2)
            ]
            crops.append((cr, ci))
            exits.append(jnp.concatenate([pr * cr - pi * ci, pr * ci + pi * cr], axis=1))
        y = dot_right(jnp.concatenate(exits, axis=0), dft[0], dft[1])

        def turn(x):
            return jnp.concatenate(
                [
                    jnp.concatenate(
                        [x[b * extent:(b + 1) * extent, c * extent:(c + 1) * extent] for b in range(2 * batch)], axis=1
                    )
                    for c in range(2)
                ],
                axis=0,
            )

        z = dot_left(dft[2], dft[3], turn(y))
        re, im = z[:extent], z[extent:]
        measured = jnp.concatenate([recv[o, slot] for o, slot in turns], axis=1)
        misfit = re * re + im * im - measured
        v = dot_left(dft[0], dft[1], jnp.concatenate([misfit * re, misfit * im], axis=0))
        turned = jnp.concatenate(
            [
                jnp.concatenate(
                    [v[c * extent:(c + 1) * extent, b * extent:(b + 1) * extent] for c in range(2)], axis=1
                )
                for b in range(2 * batch)
            ],
            axis=0,
        )
        back = dot_right(turned, dft[2], dft[3])
        sum_re, sum_im = total[:extent], total[extent:]
        nothing = jnp.zeros((extent, tile - extent), jnp.float32)
        for b in range(2 * batch):
            row, col, weight = corners[b]
            cr, ci = crops[b]
            br = back[b * extent:(b + 1) * extent, :extent] * weight
            bi = back[b * extent:(b + 1) * extent, extent:] * weight
            sum_re += cr * br + ci * bi
            sum_im += cr * bi - ci * br
            for c, term in enumerate((pr * br + pi * bi, pr * bi - pi * br)):
                wide = pltpu.roll(jnp.concatenate([term, nothing], axis=1), col, 1)
                for h in range(halves):
                    pad[b, c, h, tile - extent:tile, :] = wide[:, h * extent:(h + 1) * extent]
        total[:extent] = sum_re
        total[extent:] = sum_im
        for c in range(2):
            for start in range(0, tile, 64):
                for h in range(halves):
                    held = grad[c, start:start + 64, h * extent:(h + 1) * extent]
                    for b in range(2 * batch):
                        held += pad[b, c, h, pl.ds(tile - extent - corners[b][0] + start, 64), :]
                    grad[c, start:start + 64, h * extent:(h + 1) * extent] = held
        return carry

    lax.fori_loop(0, total_steps, step_of, 0)
    grad_copy = pltpu.make_async_copy(grad, grad_hbm, local_sem.at[0])
    grad_copy.start()

    def when(condition, body):
        if owners == members:
            body()
        else:
            pl.when(condition)(body)

    def part_of(place):
        return pl.ds(pl.multiple_of(place * rows, rows), rows)

    def scatter(step, carry):
        to = other(step)

        def go():
            pltpu.make_async_remote_copy(
                src_ref=total.at[part_of(to)], dst_ref=arrived.at[step - 1], send_sem=rs_send, recv_sem=rs_recv,
                device_id=member(to), device_id_type=MESH,
            ).start()

        when(to < owners, go)
        return carry

    def wait_for(sem, count):
        whole = arrived.at[pl.ds(0, count)]
        pltpu.make_async_copy(whole, whole, sem).wait()

    each_member(scatter)

    def gather():
        wait_for(rs_recv, members - 1)
        held = total[part_of(mine), :]
        held = held + jnp.sum(arrived[...], axis=0)
        reduced[...] = held * (1.0 / inten.shape[0])
        gathered[mine] = reduced[...]

        def tell(step, carry):
            pltpu.make_async_remote_copy(
                src_ref=reduced, dst_ref=gathered.at[mine], send_sem=ag_send, recv_sem=ag_recv,
                device_id=member(other(step)), device_id_type=MESH,
            ).start()
            return carry

        each_member(tell)

    when(mine < owners, gather)
    if owners == members:
        wait_for(ag_recv, members - 1)
        wait_for(rs_send, members - 1)
        wait_for(ag_send, members - 1)
    else:

        @pl.when(mine < owners)
        def _():
            wait_for(ag_recv, owners - 1)
            wait_for(rs_send, owners - 1)
            wait_for(ag_send, members - 1)

        @pl.when(mine >= owners)
        def _():
            wait_for(ag_recv, owners)
            wait_for(rs_send, owners)

    for place in range(owners):
        probe_out[place * rows:(place + 1) * rows] = gathered[place]
    waited = [turn for i in range(groups, total_steps - AHEAD) for turn in pair_of(i)]
    for o in range(1, n):
        for g in range(groups):
            if (o, g) not in waited:
                data_copy(o, g, me).wait_send()
    grad_copy.wait()
    for o in range(1, n):
        for copy in meta_copies(o, me):
            copy.wait_send()


def shards(object_field, probe_field, intensity, positions, owner_tile):
    n, stripes, subs = lax.axis_size("scan"), lax.axis_size("stripe"), lax.axis_size("sub")
    count, extent = intensity.shape[0], probe_field.shape[1]
    tile = object_field.shape[1]
    cap = min(count, 2 * count // n)
    batch = min(cap, 2)
    members = n * stripes * subs
    rows = max(8, 2 * extent // members)
    owners = 2 * extent // rows

    hbm = pl.BlockSpec(memory_space=pltpu.HBM)
    vmem = pl.BlockSpec(memory_space=pltpu.VMEM)
    dma = pltpu.SemaphoreType.DMA
    f32 = jnp.float32
    grad, probe_grad = pl.pallas_call(
        functools.partial(kernel, (n, stripes, subs, cap, batch)),
        out_shape=(
            jax.ShapeDtypeStruct((2, tile, tile), f32),
            jax.ShapeDtypeStruct((2 * extent, extent), f32),
        ),
        in_specs=[hbm] * 6,
        out_specs=(hbm, vmem),
        scratch_shapes=[
            pltpu.VMEM((2, tile, tile), f32),
            pltpu.VMEM(intensity.shape, f32),
            pltpu.VMEM(probe_field.shape, f32),
            pltpu.VMEM((2, extent, extent), f32),
            pltpu.VMEM((4, 2 * extent, 2 * extent), jnp.bfloat16),
            pltpu.VMEM((n, cap, extent, extent), f32),
            pltpu.VMEM((n, cap, extent, extent), f32),
            pltpu.VMEM((n, 2, count), jnp.int32),
            pltpu.VMEM((n, 1, count), jnp.int32),
            pltpu.SMEM((n, 2, count), jnp.int32),
            pltpu.SMEM((n, 1, count), jnp.int32),
            pltpu.VMEM((2, tile // extent, tile, extent), f32),
            pltpu.VMEM((2 * batch, 2, tile // extent, 2 * tile - extent, extent), f32),
            pltpu.VMEM((2 * extent, extent), f32),
            pltpu.VMEM((rows, extent), f32),
            pltpu.VMEM((owners, rows, extent), f32),
            pltpu.VMEM((members - 1, rows, extent), f32),
            dma((3 + tile // extent,)), dma((n, cap // batch)), dma((n, cap // batch)), dma((2, n)), dma((2, n)), dma((2,)), dma, dma, dma, dma,
        ],
        compiler_params=pltpu.CompilerParams(
            collective_id=0, has_side_effects=True, vmem_limit_bytes=64 * 1024 * 1024
        ),
        cost_estimate=pl.CostEstimate(
            flops=3 * 4 * 2 * 256 * 256 * 128 * n * cap, bytes_accessed=8 * 1024 * 1024, transcendentals=0
        ),
    )(positions.T, owner_tile.T, intensity, object_field, probe_field, jnp.asarray(tables(extent)))
    return grad, probe_grad.reshape(2, extent, extent)


def solution(mesh):
    in_specs = (
        P(None, ("groups", "stripe", "sub"), "scan"),
        P(None, "groups", None),
        P(("groups", "scan", "stripe", "sub"), None, None),
        P(("groups", "scan", "stripe", "sub"), None),
        P(("groups", "scan", "stripe", "sub"), None),
    )
    out_specs = (P(None, ("groups", "stripe", "sub"), "scan"), P(None, "groups", None))
    return jax.shard_map(shards, mesh=mesh, in_specs=in_specs, out_specs=out_specs, check_vma=False)
```
